32 devices in a mesh: rows: 8 (over z, y), rep: 4 (over x, core).
Axes of the slice: x: 2, y: 2, z: 4, core: 2. Of those that a mesh axis runs over, the one named last changes fastest.
Arguments:
- features: bfloat16 [16384, 128], P('rows')
- weight: bfloat16 [128, 128], replicated, may hold values from -0.5 to 0.5
- bias: float32 [128], replicated, may hold values from -3 to 3
- grad_out: bfloat16 [16384, 128], P('rows')
- tile_values: bfloat16 [8, 4, 128, 64, 64], P('rows', 'rep')
- tile_rows: int32 [8, 4, 128], P('rows', 'rep'), may hold values from 0 to 31
- tile_cols: int32 [8, 4, 128], P('rows', 'rep'), may hold values from 0 to 255, as said below
- tile_count: int32 [8, 4], P('rows', 'rep'), may hold values from 2 to 128, as said below
Outputs:
- hidden: bfloat16 [16384, 128], P('rows')
- grad_w: float32 [128, 128], replicated
- grad_b: float32 [128], replicated
The draws below stay inside these ranges and needn't reach their ends.
Inputs may be any that keep to these rules, and one draw needn't show every extreme that they name: tile_count is 128 on some device in every draw. tile_cols[i, j, t] // 32 is a row block k with k % 4 == j.
All inputs are finite; a program needn't handle non-finite values.
Results may differ from the reference program's by a relative error of at most 0.007.
Values may be sent and summed in bfloat16 or wider, within the bound.
A program may use at most 64 MiB of HBM per device.

```python
import math
import jax
import jax.numpy as jnp
from jax import lax

FEAT = 128
TILE = 64
TILE_ROWS = 32
TILES_MAX = 128
BLOCKS = 8
COPIES = 4
SECTIONS = 2
NODES = 16384
NTILES = 256


def layout(key):
    base_key = jax.random.fold_in(key, 7)
    subkeys = jax.random.split(base_key, 6)
    porosity = jax.random.randint(subkeys[0], (BLOCKS, 1), 1, 5)
    rising = COPIES - 1 + 2 * jnp.arange(COPIES, dtype=jnp.int32)
    planned = TILES_MAX * porosity * rising[None, :] // (4 * (3 * COPIES - 3))
    jitter = jax.random.randint(subkeys[1], (BLOCKS, COPIES), 0, TILES_MAX // 8 + 1)
    counts = jnp.clip(planned - jitter, 2, TILES_MAX)
    chosen = jax.random.randint(subkeys[2], (), 0, BLOCKS)
    picked = (jnp.arange(BLOCKS)[:, None] == chosen) & (jnp.arange(COPIES)[None, :] == COPIES - 1)
    counts = jnp.where(picked, TILES_MAX, counts).astype(jnp.int32)
    row_ids = jax.random.randint(subkeys[3], (BLOCKS, COPIES, TILES_MAX), 0, TILE_ROWS)
    section_ids = jax.random.randint(subkeys[4], (BLOCKS, COPIES, TILES_MAX), 0, SECTIONS)
    offsets = jax.random.randint(subkeys[5], (BLOCKS, COPIES, TILES_MAX), 0, TILE_ROWS)
    class_ids = jnp.arange(COPIES, dtype=jnp.int32)[None, :, None]
    col_ids = (section_ids * COPIES + class_ids) * TILE_ROWS + offsets
    first_slot = picked[:, :, None] & (jnp.arange(TILES_MAX)[None, None, :] == 0)
    row_ids = jnp.where(first_slot, TILE_ROWS - 1, row_ids).astype(jnp.int32)
    col_ids = jnp.where(first_slot, NTILES - 1, col_ids).astype(jnp.int32)
    return (counts, row_ids, col_ids)


def draw_tile_count(key, part):
    return layout(key)[0]


def draw_tile_rows(key, part):
    return layout(key)[1]


def draw_tile_cols(key, part):
    return layout(key)[2]


def draw_tile_values(key, part):
    value_key = jax.random.fold_in(key, 9)

    def one_block(block_index):
        block_key = jax.random.fold_in(value_key, block_index)
        first_key, second_key = jax.random.split(block_key, 2)
        occupied = jax.random.uniform(first_key, (COPIES, TILES_MAX, TILE, TILE), jnp.float32) < 0.013
        strength = jax.random.uniform(second_key, (COPIES, TILES_MAX, TILE, TILE), jnp.float32, 0.2, 2.0)
        return (occupied.astype(jnp.float32) * strength).astype(jnp.bfloat16)
    return lax.map(one_block, jnp.arange(BLOCKS, dtype=jnp.int32))


def draw_features(key, part):
    first_key, second_key = jax.random.split(jax.random.fold_in(key, 3), 2)
    feature_mean = jax.random.uniform(first_key, (FEAT,), jnp.float32, -1.5, 1.5)
    fluctuation = jax.random.normal(second_key, (NODES, FEAT), jnp.float32)
    return (feature_mean[None, :] + fluctuation).astype(jnp.bfloat16)


def draw_grad_out(key, part):
    first_key = jax.random.fold_in(jax.random.fold_in(key, 5), 0)
    rising_scale = 1.0 + 2.0 * jnp.arange(NODES, dtype=jnp.float32) / (NODES - 1)
    fluctuation = jax.random.normal(first_key, (NODES, FEAT), jnp.float32)
    return (fluctuation * rising_scale[:, None] / math.sqrt(NODES)).astype(jnp.bfloat16)


def centred(rng, extent, spread, bound, kind=jnp.bfloat16):
    array = spread * jax.random.normal(rng, extent, jnp.float32)
    return jnp.clip(array, min=-bound, max=bound).astype(kind)


def setup_inputs(seed: int = 0) -> dict:
    keys = jax.random.split(jax.random.key(seed), 9)
    features = draw_features(jax.random.fold_in(keys[8], 71), 0)
    weight = centred(keys[1], (FEAT, FEAT), FEAT ** -0.5, 0.5)
    bias = centred(keys[2], (FEAT,), 0.5, 3.0, jnp.float32)
    grad_out = draw_grad_out(jax.random.fold_in(keys[8], 71), 0)
    tile_values = draw_tile_values(jax.random.fold_in(keys[8], 71), 0)
    tile_rows = draw_tile_rows(jax.random.fold_in(keys[8], 71), 0)
    tile_cols = draw_tile_cols(jax.random.fold_in(keys[8], 71), 0)
    tile_count = draw_tile_count(jax.random.fold_in(keys[8], 71), 0)
    return dict(features=features, weight=weight, bias=bias, grad_out=grad_out, tile_values=tile_values, tile_rows=tile_rows, tile_cols=tile_cols, tile_count=tile_count)


def reference(features, weight, bias, grad_out, tile_values, tile_rows, tile_cols, tile_count):
    slot_ids = jnp.arange(TILES_MAX, dtype=jnp.int32)
    live_mask = slot_ids[None, None, :] < tile_count[:, :, None]
    flat_values = tile_values.reshape(BLOCKS * COPIES, TILES_MAX, TILE, TILE)
    flat_live = live_mask.reshape(BLOCKS * COPIES, TILES_MAX)
    flat_rows = tile_rows.reshape(BLOCKS * COPIES, TILES_MAX)
    flat_cols = tile_cols.reshape(BLOCKS * COPIES, TILES_MAX)
    owners = (jnp.arange(BLOCKS * COPIES, dtype=jnp.int32) // COPIES).astype(jnp.int32)

    def add_degree(running, scanned):
        values, alive_mask, row_ids, owner_block = scanned
        row_sums = lax.optimization_barrier(jnp.sum(values.astype(jnp.float32), axis=2))
        row_sums = jnp.where(alive_mask[:, None], row_sums, jnp.float32(0.0))
        return (running.at[owner_block, row_ids].add(row_sums), None)
    start_degree = jnp.zeros((BLOCKS, TILE_ROWS, TILE), jnp.float32)
    degree = lax.scan(add_degree, start_degree, (flat_values, flat_live, flat_rows, owners))[0]
    inv_root = lax.rsqrt(1.0 + degree.reshape(NODES))
    scaled = (features.astype(jnp.float32) * inv_root[:, None]).astype(jnp.bfloat16)
    tiles_x = scaled.reshape(NTILES, TILE, FEAT)

    def add_products(running, scanned):
        values, alive_mask, row_ids, col_ids, owner_block = scanned
        values = jnp.where(alive_mask[:, None, None], values.astype(jnp.float32), jnp.float32(0.0))
        gathered = tiles_x[col_ids].astype(jnp.float32)
        products = jnp.einsum('tab,tbf->taf', values, gathered)
        return (running.at[owner_block, row_ids].add(products), None)
    start_sum = jnp.zeros((BLOCKS, TILE_ROWS, TILE, FEAT), jnp.float32)
    aggregated = lax.scan(add_products, start_sum, (flat_values, flat_live, flat_rows, flat_cols, owners))[0]
    aggregated = aggregated.reshape(NODES, FEAT)
    smoothed = (inv_root[:, None] * (aggregated + scaled.astype(jnp.float32))).astype(jnp.bfloat16)
    preact = jnp.dot(smoothed, weight, preferred_element_type=jnp.float32) + bias
    hidden = jax.nn.silu(preact).astype(jnp.bfloat16)
    sigmoid_pre = jax.nn.sigmoid(preact)
    silu_slope = sigmoid_pre * (1.0 + preact * (1.0 - sigmoid_pre))
    grad_pre = grad_out.astype(jnp.float32) * silu_slope
    grad_b = lax.optimization_barrier(jnp.sum(grad_pre, axis=0))
    grad_low = grad_pre.astype(jnp.bfloat16)
    grad_w = lax.dot_general(smoothed, grad_low, (((0,), (0,)), ((), ())), preferred_element_type=jnp.float32)
    return (hidden, grad_w, grad_b)
```

```python
import functools
import jax
import jax.numpy as jnp
from jax import lax
from jax.experimental import pallas as pl
from jax.experimental.pallas import tpu as pltpu
from jax.sharding import PartitionSpec as P

MESH = pl.DeviceIdType.MESH
CHUNKS = 4
GROUP = 8


def spread_kernel(R, C, S, feat, ldeg, buf, deg_x, deg_o, send_f, recv_f, send_x, recv_x, send_o, recv_o):
    r = lax.axis_index("rows")
    j = lax.axis_index("rep")
    z = r // 2
    y = r % 2
    Z = R // 2
    rows = feat.shape[0] // CHUNKS

    barrier = pltpu.get_barrier_semaphore()

    def greet(d, carry):
        who = (r * C + j + d) % (R * C)
        pl.semaphore_signal(barrier, inc=1, device_id=(who // C, who % C), device_id_type=MESH)
        return carry

    lax.fori_loop(1, R * C, greet, 0)
    pl.semaphore_wait(barrier, R * C - 1)

    def feature_copy(s, c, way, target, own):
        dst = buf.at[s, pl.ds(c * rows, rows)]
        src = feat.at[pl.ds(c * rows, rows)] if own else dst
        return pltpu.make_async_remote_copy(
            src_ref=src, dst_ref=dst, send_sem=send_f.at[s, c, way], recv_sem=recv_f.at[s, c],
            device_id=(target, j), device_id_type=MESH)

    def ways(s):
        k = s * C + j
        zs = k // 2
        on_column = y == k % 2
        return (
            (0, jnp.logical_and(on_column, jnp.logical_and(z >= zs, z < Z - 1)), r + 2),
            (1, jnp.logical_and(on_column, jnp.logical_and(z <= zs, z > 0)), r - 2),
            (2, on_column, r + 1 - 2 * y),
        )

    for c in range(CHUNKS):
        for s in range(S):
            for way, active, target in ways(s):
                @pl.when(jnp.logical_and(active, r == s * C + j))
                def _():
                    feature_copy(s, c, way, target, True).start()

    home = r % C
    section = r // C

    def degree_copy(d):
        return pltpu.make_async_remote_copy(
            src_ref=ldeg, dst_ref=deg_x.at[section, j], send_sem=send_x.at[d], recv_sem=recv_x.at[section, j],
            device_id=((r + d) % R, home), device_id_type=MESH)

    for d in range(R):
        if d == 0:
            @pl.when(j != home)
            def _():
                degree_copy(0).start()

            @pl.when(j == home)
            def _():
                deg_x[section, j] = ldeg[...]
        else:
            degree_copy(d).start()
    for d in range(1, C):
        pltpu.make_async_remote_copy(
            src_ref=ldeg, dst_ref=deg_o.at[j], send_sem=send_o.at[d], recv_sem=recv_o.at[j],
            device_id=(r, (j + d) % C), device_id_type=MESH).start()
    deg_o[j] = ldeg[...]

    for s in range(S):
        @pl.when(r == s * C + j)
        def _():
            buf[s] = feat[...]

    for c in range(CHUNKS):
        for s in range(S):
            @pl.when(r != s * C + j)
            def _():
                feature_copy(s, c, 0, (r + 1) % R, False).wait_recv()
            for way, active, target in ways(s):
                @pl.when(jnp.logical_and(active, r != s * C + j))
                def _():
                    feature_copy(s, c, way, target, False).start()

    for s in range(S):
        for a in range(C):
            @pl.when(jnp.logical_or(r != s * C + j, a != j))
            def _():
                pltpu.make_async_remote_copy(
                    src_ref=ldeg, dst_ref=deg_x.at[s, a], send_sem=send_x.at[0], recv_sem=recv_x.at[s, a],
                    device_id=((r + 1) % R, j), device_id_type=MESH).wait_recv()
    for d in range(1, C):
        a = (j + d) % C
        copy = pltpu.make_async_remote_copy(
            src_ref=ldeg, dst_ref=deg_o.at[a], send_sem=send_o.at[d], recv_sem=recv_o.at[a],
            device_id=(r, a), device_id_type=MESH)
        copy.wait_recv()
        copy.wait_send()
    for d in range(R):
        if d == 0:
            @pl.when(j != home)
            def _():
                degree_copy(0).wait_send()
        else:
            degree_copy(d).wait_send()
    for c in range(CHUNKS):
        for s in range(S):
            for way, active, target in ways(s):
                @pl.when(active)
                def _():
                    feature_copy(s, c, way, target, False).wait_send()


def tile_kernel(tiles, tile, row_ids, index, count, values, buf, out, total):
    total[...] = jnp.zeros_like(total)
    live = count[0]

    def group(number, carry):
        products = []
        for u in range(GROUP):
            t = number * GROUP + u
            start = pl.multiple_of(index[t] * tile, tile)
            products.append(
                jnp.dot(values[t], buf[pl.ds(start, tile)], preferred_element_type=jnp.float32))
        for u in range(GROUP):
            t = number * GROUP + u
            row = jnp.where(t < live, row_ids[t], tiles)
            place = pl.ds(pl.multiple_of(row * tile, tile), tile)
            total[place] = total[place] + products[u]
        return carry

    lax.fori_loop(0, (live + GROUP - 1) // GROUP, group, 0)
    out[...] = total[: tiles * tile].astype(out.dtype)


def dense_kernel(R, C, part, scaled, inv, grad_out, weight, bias, hidden, grad_w, grad_b,
                 arrived, g1, g1_in, g2_in, low,
                 send_p, recv_p, send_h, recv_h, send_1, recv_1, send_2, recv_2, send_w, recv_w):
    r = lax.axis_index("rows")
    j = lax.axis_index("rep")
    barrier = pltpu.get_barrier_semaphore()
    for d in range(1, C):
        pl.semaphore_signal(barrier, inc=1, device_id=(r, (j + d) % C), device_id_type=MESH)
    for d in range(1, R):
        pl.semaphore_signal(barrier, inc=1, device_id=((r + d) % R, j), device_id_type=MESH)
    pl.semaphore_wait(barrier, R + C - 2)

    def to_rep(d, src, dst, send, recv):
        return pltpu.make_async_remote_copy(
            src_ref=src, dst_ref=dst.at[j], send_sem=send.at[d], recv_sem=recv.at[j],
            device_id=(r, (j + d) % C), device_id_type=MESH)

    def from_rep(d, dst, send, recv):
        a = (j + d) % C
        return pltpu.make_async_remote_copy(
            src_ref=dst.at[a], dst_ref=dst.at[a], send_sem=send.at[d], recv_sem=recv.at[a],
            device_id=(r, a), device_id_type=MESH)

    for d in range(1, C):
        to_rep(d, part.at[(j + d) % C], arrived, send_p, recv_p).start()
    summed = part[j].astype(jnp.float32) + scaled[...].astype(jnp.float32)
    for d in range(1, C):
        from_rep(d, arrived, send_p, recv_p).wait_recv()
        summed = summed + arrived[(j + d) % C].astype(jnp.float32)
    smoothed = (inv[...] * summed).astype(jnp.bfloat16)
    preact = jnp.dot(smoothed, weight[...], preferred_element_type=jnp.float32) + bias[...]
    sig = 1.0 / (1.0 + jnp.exp(-preact))
    hidden[j] = (preact * sig).astype(jnp.bfloat16)
    for d in range(1, C):
        to_rep(d, hidden.at[j], hidden, send_h, recv_h).start()
    grad_pre = grad_out[...].astype(jnp.float32) * (sig * (1.0 + preact * (1.0 - sig)))
    gb = jnp.sum(grad_pre, axis=0, keepdims=True)
    gw = lax.dot_general(smoothed, grad_pre.astype(jnp.bfloat16), (((0,), (0,)), ((), ())),
                         preferred_element_type=jnp.float32)
    share = gw.shape[0] // C
    for a in range(C):
        g1[a, :share] = gw[a * share:(a + 1) * share]
        g1[a, share:] = jnp.broadcast_to(gb, (8, gb.shape[1]))
    for d in range(1, C):
        to_rep(d, g1.at[(j + d) % C], g1_in, send_1, recv_1).start()
    g1_in[j] = g1[j]
    for d in range(1, C):
        from_rep(d, g1_in, send_1, recv_1).wait_recv()
    mine = g1_in[0]
    for a in range(1, C):
        mine = mine + g1_in[a]
    low[...] = mine

    def to_rows(d):
        return pltpu.make_async_remote_copy(
            src_ref=low, dst_ref=g2_in.at[r], send_sem=send_2.at[d], recv_sem=recv_2.at[r],
            device_id=((r + d) % R, j), device_id_type=MESH)

    for d in range(1, R):
        to_rows(d).start()
    g2_in[r] = mine
    for d in range(1, R):
        a = (r + d) % R
        pltpu.make_async_remote_copy(
            src_ref=low, dst_ref=g2_in.at[a], send_sem=send_2.at[d], recv_sem=recv_2.at[a],
            device_id=(a, j), device_id_type=MESH).wait_recv()
    whole = g2_in[0]
    for a in range(1, R):
        whole = whole + g2_in[a]
    grad_w[j] = whole[:share]
    grad_b[...] = whole[share:share + 1]
    for d in range(1, C):
        to_rep(d, grad_w.at[j], grad_w, send_w, recv_w).start()
    for d in range(1, C):
        from_rep(d, grad_w, send_w, recv_w).wait_recv()
        from_rep(d, hidden, send_h, recv_h).wait_recv()
    for d in range(1, C):
        to_rep(d, part.at[(j + d) % C], arrived, send_p, recv_p).wait_send()
        to_rep(d, hidden.at[j], hidden, send_h, recv_h).wait_send()
        to_rep(d, g1.at[(j + d) % C], g1_in, send_1, recv_1).wait_send()
        to_rep(d, grad_w.at[j], grad_w, send_w, recv_w).wait_send()
    for d in range(1, R):
        to_rows(d).wait_send()


def local(features, weight, bias, grad_out, tile_values, tile_rows, tile_cols, tile_count):
    values = tile_values[0, 0]
    row_ids = tile_rows[0, 0]
    col_ids = tile_cols[0, 0]
    live_count = tile_count[0, 0]
    N, F = features.shape
    T, tile = values.shape[0], values.shape[1]
    tiles = N // tile
    R = lax.axis_size("rows")
    C = lax.axis_size("rep")
    S = R // C
    j = lax.axis_index("rep")
    vmem = pl.BlockSpec(memory_space=pltpu.VMEM)
    smem = pl.BlockSpec(memory_space=pltpu.SMEM)
    dma = pltpu.SemaphoreType.DMA
    f32, bf16 = jnp.float32, jnp.bfloat16
    sds = jax.ShapeDtypeStruct

    row_sums = jnp.sum(values, axis=2, dtype=f32)
    place = jnp.logical_and(
        row_ids[None, :] == jnp.arange(tiles, dtype=jnp.int32)[:, None],
        jnp.arange(T, dtype=jnp.int32)[None, :] < live_count)
    local_degree = jnp.dot(place.astype(f32), row_sums, precision=lax.Precision.HIGHEST)
    ldeg = local_degree.reshape(N // 128, 128)

    buf, deg_x, deg_o = pl.pallas_call(
        functools.partial(spread_kernel, R, C, S),
        out_shape=(sds((S, N, F), bf16), sds((S, C, N // 128, 128), f32), sds((C, N // 128, 128), f32)),
        in_specs=[vmem] * 2,
        out_specs=(vmem,) * 3,
        scratch_shapes=[
            dma((S, CHUNKS, 3)), dma((S, CHUNKS)), dma((R,)), dma((S, C)), dma((C,)), dma((C,))],
        compiler_params=pltpu.CompilerParams(
            collective_id=0, has_side_effects=True, vmem_limit_bytes=32 * 2**20),
    )(features, ldeg)

    inv_x = lax.rsqrt(1.0 + jnp.sum(deg_x, axis=1).reshape(S, N))
    scaled_x = (buf.astype(f32) * inv_x[:, :, None]).astype(bf16).reshape(S * N, F)
    inv_o = lax.rsqrt(1.0 + jnp.sum(deg_o, axis=0).reshape(N))
    column_block = col_ids // tiles
    local_index = column_block // C * tiles + col_ids % tiles

    part = pl.pallas_call(
        functools.partial(tile_kernel, tiles, tile),
        out_shape=sds((N, F), bf16),
        in_specs=[smem, smem, smem, vmem, vmem],
        out_specs=vmem,
        scratch_shapes=[pltpu.VMEM(((tiles + 1) * tile, F), f32)],
        compiler_params=pltpu.CompilerParams(vmem_limit_bytes=32 * 2**20),
    )(row_ids, local_index, live_count[None], values, scaled_x)

    q = N // C
    own_inv = jnp.broadcast_to(lax.dynamic_slice_in_dim(inv_o, j * q, q)[:, None], (q, F))
    own_scaled = (lax.dynamic_slice_in_dim(features, j * q, q).astype(f32) * own_inv).astype(bf16)
    own_grad = lax.dynamic_slice_in_dim(grad_out, j * q, q)
    share = F // C
    hidden, grad_w, grad_b = pl.pallas_call(
        functools.partial(dense_kernel, R, C),
        out_shape=(sds((C, q, F), bf16), sds((C, share, F), f32), sds((1, F), f32)),
        in_specs=[vmem] * 6,
        out_specs=(vmem,) * 3,
        scratch_shapes=[
            pltpu.VMEM((C, q, F), bf16),
            pltpu.VMEM((C, share + 8, F), f32),
            pltpu.VMEM((C, share + 8, F), f32),
            pltpu.VMEM((R, share + 8, F), f32),
            pltpu.VMEM((share + 8, F), f32),
            dma((C,)), dma((C,)), dma((C,)), dma((C,)), dma((C,)), dma((C,)), dma((R,)), dma((R,)),
            dma((C,)), dma((C,))],
        compiler_params=pltpu.CompilerParams(
            collective_id=1, has_side_effects=True, vmem_limit_bytes=32 * 2**20),
    )(part.reshape(C, q, F), own_scaled, own_inv, own_grad, weight, bias[None, :])
    return (hidden.reshape(N, F), grad_w.reshape(F, F), grad_b.reshape(F))


def solution(mesh):
    return jax.shard_map(
        local,
        mesh=mesh,
        in_specs=(
            P("rows", None),
            P(),
            P(),
            P("rows", None),
            P("rows", "rep", None, None, None),
            P("rows", "rep", None),
            P("rows", "rep", None),
            P("rows", "rep"),
        ),
        out_specs=(P("rows", None), P(), P()),
        check_vma=False,
    )
```

```python
import functools
import jax
import jax.numpy as jnp
from jax import lax
from jax.experimental import pallas as pl
from jax.experimental.pallas import tpu as pltpu
from jax.sharding import PartitionSpec as P

MESH = pl.DeviceIdType.MESH
CHUNKS = 16
GROUP = 8


def spread_kernel(R, C, S, feat, ldeg, buf, deg_x, deg_o, deg_in, send_f, recv_f, send_x, recv_x, send_o, recv_o):
    r = lax.axis_index("rows")
    j = lax.axis_index("rep")
    z = r // 2
    y = r % 2
    Z = R // 2
    rows = feat.shape[0] // CHUNKS
    neighbours = ((z < Z - 1, r + 2), (z > 0, r - 2))

    barrier = pltpu.get_barrier_semaphore()
    for d in range(1, C):
        pl.semaphore_signal(barrier, inc=1, device_id=(r, (j + d) % C), device_id_type=MESH)
    pl.semaphore_signal(barrier, inc=1, device_id=(r + 1 - 2 * y, j), device_id_type=MESH)
    for there, target in neighbours:
        @pl.when(there)
        def _():
            pl.semaphore_signal(barrier, inc=1, device_id=(target, j), device_id_type=MESH)
    pl.semaphore_wait(barrier, C + jnp.where(z < Z - 1, 1, 0) + jnp.where(z > 0, 1, 0))

    def feature_copy(s, c, way, target, own):
        place = pl.ds(pl.multiple_of(c * rows, rows), rows)
        dst = buf.at[s, place]
        return pltpu.make_async_remote_copy(
            src_ref=feat.at[place] if own else dst, dst_ref=dst,
            send_sem=send_f.at[s, c, way], recv_sem=recv_f.at[s, c],
            device_id=(target, j), device_id_type=MESH)

    def degree_copy(s, way, target):
        return pltpu.make_async_remote_copy(
            src_ref=deg_x.at[s], dst_ref=deg_x.at[s], send_sem=send_x.at[s, way], recv_sem=recv_x.at[s],
            device_id=(target, j), device_id_type=MESH)

    def ways(s):
        k = s * C + j
        zs = k // 2
        on_column = y == k % 2
        return (
            (0, jnp.logical_and(on_column, jnp.logical_and(z >= zs, z < Z - 1)), r + 2),
            (1, jnp.logical_and(on_column, jnp.logical_and(z <= zs, z > 0)), r - 2),
            (2, on_column, r + 1 - 2 * y),
        )

    def each_chunk(body):
        def step(c, carry):
            body(c)
            return carry
        lax.fori_loop(0, CHUNKS, step, 0)

    for d in range(1, C):
        pltpu.make_async_remote_copy(
            src_ref=ldeg, dst_ref=deg_in.at[j], send_sem=send_o.at[d], recv_sem=recv_o.at[j],
            device_id=(r, (j + d) % C), device_id_type=MESH).start()

    for s in range(S):
        @pl.when(r == s * C + j)
        def _():
            def send_chunk(c):
                for way, active, target in ways(s):
                    @pl.when(active)
                    def _():
                        feature_copy(s, c, way, target, True).start()
            each_chunk(send_chunk)

    deg_in[j] = ldeg[...]
    for d in range(1, C):
        a = (j + d) % C
        pltpu.make_async_remote_copy(
            src_ref=ldeg, dst_ref=deg_in.at[a], send_sem=send_o.at[d], recv_sem=recv_o.at[a],
            device_id=(r, a), device_id_type=MESH).wait_recv()
    degree = deg_in[0]
    for a in range(1, C):
        degree = degree + deg_in[a]
    deg_o[...] = degree

    for s in range(S):
        @pl.when(r == s * C + j)
        def _():
            deg_x[s] = degree
            for way, active, target in ways(s):
                @pl.when(active)
                def _():
                    degree_copy(s, way, target).start()
            buf[s] = feat[...]

    gaps = [jnp.abs(z - (s * C + j) // 2) for s in range(S)]
    ranks = []
    for s in range(S):
        rank = 0
        for t in range(S):
            if t != s:
                ahead = gaps[t] <= gaps[s] if t < s else gaps[t] < gaps[s]
                rank = rank + jnp.where(ahead, 1, 0)
        ranks.append(rank)
    for i in range(S):
        for s in range(S):
            @pl.when(jnp.logical_and(ranks[s] == i, r != s * C + j))
            def _():
                def pass_chunk(c):
                    feature_copy(s, c, 0, r + 1 - 2 * y, False).wait_recv()
                    for way, active, target in ways(s):
                        @pl.when(active)
                        def _():
                            feature_copy(s, c, way, target, False).start()
                each_chunk(pass_chunk)
                degree_copy(s, 0, r + 1 - 2 * y).wait_recv()
                for way, active, target in ways(s):
                    @pl.when(active)
                    def _():
                        degree_copy(s, way, target).start()

    for d in range(1, C):
        pltpu.make_async_remote_copy(
            src_ref=ldeg, dst_ref=deg_in.at[j], send_sem=send_o.at[d], recv_sem=recv_o.at[j],
            device_id=(r, (j + d) % C), device_id_type=MESH).wait_send()
    for s in range(S):
        for way, active, target in ways(s):
            @pl.when(active)
            def _():
                each_chunk(lambda c: feature_copy(s, c, way, target, False).wait_send())
                degree_copy(s, way, target).wait_send()


def tile_kernel(tiles, tile, row_ids, index, count, values, buf, out, total):
    total[...] = jnp.zeros_like(total)
    live = count[0]

    def group(number, carry):
        products = []
        for u in range(GROUP):
            t = number * GROUP + u
            start = pl.multiple_of(index[t] * tile, tile)
            products.append(
                jnp.dot(values[t], buf[pl.ds(start, tile)], preferred_element_type=jnp.float32))
        for u in range(GROUP):
            t = number * GROUP + u
            row = jnp.where(t < live, row_ids[t], tiles)
            place = pl.ds(pl.multiple_of(row * tile, tile), tile)
            total[place] = total[place] + products[u]
        return carry

    lax.fori_loop(0, (live + GROUP - 1) // GROUP, group, 0)
    out[...] = total[: tiles * tile].astype(out.dtype)


def dense_kernel(R, C, part, scaled, inv, grad_out, weight, bias, hidden, grad_w, grad_b,
                 arrived, g1, g1_in, g2_in, low,
                 send_p, recv_p, send_h, recv_h, send_1, recv_1, send_2, recv_2, send_w, recv_w):
    r = lax.axis_index("rows")
    j = lax.axis_index("rep")
    barrier = pltpu.get_barrier_semaphore()
    for d in range(1, C):
        pl.semaphore_signal(barrier, inc=1, device_id=(r, (j + d) % C), device_id_type=MESH)
    for d in range(1, R):
        pl.semaphore_signal(barrier, inc=1, device_id=((r + d) % R, j), device_id_type=MESH)
    pl.semaphore_wait(barrier, R + C - 2)

    def to_rep(d, src, dst, send, recv):
        return pltpu.make_async_remote_copy(
            src_ref=src, dst_ref=dst.at[j], send_sem=send.at[d], recv_sem=recv.at[j],
            device_id=(r, (j + d) % C), device_id_type=MESH)

    def from_rep(d, dst, send, recv):
        a = (j + d) % C
        return pltpu.make_async_remote_copy(
            src_ref=dst.at[a], dst_ref=dst.at[a], send_sem=send.at[d], recv_sem=recv.at[a],
            device_id=(r, a), device_id_type=MESH)

    for d in range(1, C):
        to_rep(d, part.at[(j + d) % C], arrived, send_p, recv_p).start()
    summed = part[j].astype(jnp.float32) + scaled[...].astype(jnp.float32)
    for d in range(1, C):
        from_rep(d, arrived, send_p, recv_p).wait_recv()
        summed = summed + arrived[(j + d) % C].astype(jnp.float32)
    smoothed = (inv[...] * summed).astype(jnp.bfloat16)
    preact = jnp.dot(smoothed, weight[...], preferred_element_type=jnp.float32) + bias[...]
    sig = 1.0 / (1.0 + jnp.exp(-preact))
    hidden[j] = (preact * sig).astype(jnp.bfloat16)
    grad_pre = grad_out[...].astype(jnp.float32) * (sig * (1.0 + preact * (1.0 - sig)))
    gb = jnp.sum(grad_pre, axis=0, keepdims=True)
    gw = lax.dot_general(smoothed, grad_pre.astype(jnp.bfloat16), (((0,), (0,)), ((), ())),
                         preferred_element_type=jnp.float32)
    share = gw.shape[0] // C
    for a in range(C):
        g1[a, :share] = gw[a * share:(a + 1) * share]
        g1[a, share:] = jnp.broadcast_to(gb, (8, gb.shape[1]))
    for d in range(1, C):
        to_rep(d, g1.at[(j + d) % C], g1_in, send_1, recv_1).start()
    for d in range(1, C):
        to_rep(d, hidden.at[j], hidden, send_h, recv_h).start()
    g1_in[j] = g1[j]
    for d in range(1, C):
        from_rep(d, g1_in, send_1, recv_1).wait_recv()
    mine = g1_in[0]
    for a in range(1, C):
        mine = mine + g1_in[a]
    low[...] = mine

    def to_rows(d):
        return pltpu.make_async_remote_copy(
            src_ref=low, dst_ref=g2_in.at[r], send_sem=send_2.at[d], recv_sem=recv_2.at[r],
            device_id=((r + d) % R, j), device_id_type=MESH)

    for d in range(1, R):
        to_rows(d).start()
    g2_in[r] = mine
    for d in range(1, R):
        a = (r + d) % R
        pltpu.make_async_remote_copy(
            src_ref=low, dst_ref=g2_in.at[a], send_sem=send_2.at[d], recv_sem=recv_2.at[a],
            device_id=(a, j), device_id_type=MESH).wait_recv()
    whole = g2_in[0]
    for a in range(1, R):
        whole = whole + g2_in[a]
    grad_w[j] = whole[:share]
    grad_b[...] = whole[share:share + 1]
    for d in range(1, C):
        to_rep(d, grad_w.at[j], grad_w, send_w, recv_w).start()
    for d in range(1, C):
        from_rep(d, grad_w, send_w, recv_w).wait_recv()
        from_rep(d, hidden, send_h, recv_h).wait_recv()
    for d in range(1, C):
        to_rep(d, part.at[(j + d) % C], arrived, send_p, recv_p).wait_send()
        to_rep(d, hidden.at[j], hidden, send_h, recv_h).wait_send()
        to_rep(d, g1.at[(j + d) % C], g1_in, send_1, recv_1).wait_send()
        to_rep(d, grad_w.at[j], grad_w, send_w, recv_w).wait_send()
    for d in range(1, R):
        to_rows(d).wait_send()


def local(features, weight, bias, grad_out, tile_values, tile_rows, tile_cols, tile_count):
    values = tile_values[0, 0]
    row_ids = tile_rows[0, 0]
    col_ids = tile_cols[0, 0]
    live_count = tile_count[0, 0]
    N, F = features.shape
    T, tile = values.shape[0], values.shape[1]
    tiles = N // tile
    R = lax.axis_size("rows")
    C = lax.axis_size("rep")
    S = R // C
    j = lax.axis_index("rep")
    vmem = pl.BlockSpec(memory_space=pltpu.VMEM)
    smem = pl.BlockSpec(memory_space=pltpu.SMEM)
    dma = pltpu.SemaphoreType.DMA
    f32, bf16 = jnp.float32, jnp.bfloat16
    sds = jax.ShapeDtypeStruct

    row_sums = jnp.sum(values, axis=2, dtype=f32)
    place = jnp.logical_and(
        row_ids[None, :] == jnp.arange(tiles, dtype=jnp.int32)[:, None],
        jnp.arange(T, dtype=jnp.int32)[None, :] < live_count)
    local_degree = jnp.dot(place.astype(f32), row_sums, precision=lax.Precision.HIGHEST)
    ldeg = local_degree.reshape(N // 128, 128)

    buf, deg_x, deg_o = pl.pallas_call(
        functools.partial(spread_kernel, R, C, S),
        out_shape=(sds((S, N, F), bf16), sds((S, N // 128, 128), f32), sds((N // 128, 128), f32)),
        in_specs=[vmem] * 2,
        out_specs=(vmem,) * 3,
        scratch_shapes=[
            pltpu.VMEM((C, N // 128, 128), f32),
            dma((S, CHUNKS, 3)), dma((S, CHUNKS)), dma((S, 3)), dma((S,)), dma((C,)), dma((C,))],
        compiler_params=pltpu.CompilerParams(
            collective_id=0, has_side_effects=True, vmem_limit_bytes=32 * 2**20),
    )(features, ldeg)

    inv_x = lax.rsqrt(1.0 + deg_x.reshape(S, N))
    scaled_x = (buf.astype(f32) * inv_x[:, :, None]).astype(bf16).reshape(S * N, F)
    inv_o = lax.rsqrt(1.0 + deg_o.reshape(N))
    column_block = col_ids // tiles
    local_index = column_block // C * tiles + col_ids % tiles

    part = pl.pallas_call(
        functools.partial(tile_kernel, tiles, tile),
        out_shape=sds((N, F), bf16),
        in_specs=[smem, smem, smem, vmem, vmem],
        out_specs=vmem,
        scratch_shapes=[pltpu.VMEM(((tiles + 1) * tile, F), f32)],
        compiler_params=pltpu.CompilerParams(vmem_limit_bytes=32 * 2**20),
    )(row_ids, local_index, live_count[None], values, scaled_x)

    q = N // C
    own_inv = jnp.broadcast_to(lax.dynamic_slice_in_dim(inv_o, j * q, q)[:, None], (q, F))
    own_scaled = (lax.dynamic_slice_in_dim(features, j * q, q).astype(f32) * own_inv).astype(bf16)
    own_grad = lax.dynamic_slice_in_dim(grad_out, j * q, q)
    share = F // C
    hidden, grad_w, grad_b = pl.pallas_call(
        functools.partial(dense_kernel, R, C),
        out_shape=(sds((C, q, F), bf16), sds((C, share, F), f32), sds((1, F), f32)),
        in_specs=[vmem] * 6,
        out_specs=(vmem,) * 3,
        scratch_shapes=[
            pltpu.VMEM((C, q, F), bf16),
            pltpu.VMEM((C, share + 8, F), f32),
            pltpu.VMEM((C, share + 8, F), f32),
            pltpu.VMEM((R, share + 8, F), f32),
            pltpu.VMEM((share + 8, F), f32),
            dma((C,)), dma((C,)), dma((C,)), dma((C,)), dma((C,)), dma((C,)), dma((R,)), dma((R,)),
            dma((C,)), dma((C,))],
        compiler_params=pltpu.CompilerParams(
            collective_id=1, has_side_effects=True, vmem_limit_bytes=32 * 2**20),
    )(part.reshape(C, q, F), own_scaled, own_inv, own_grad, weight, bias[None, :])
    return (hidden.reshape(N, F), grad_w.reshape(F, F), grad_b.reshape(F))


def solution(mesh):
    return jax.shard_map(
        local,
        mesh=mesh,
        in_specs=(
            P("rows", None),
            P(),
            P(),
            P("rows", None),
            P("rows", "rep", None, None, None),
            P("rows", "rep", None),
            P("rows", "rep", None),
            P("rows", "rep"),
        ),
        out_specs=(P("rows", None), P(), P()),
        check_vma=False,
    )
```

```python
import functools
import jax
import jax.numpy as jnp
from jax import lax
from jax.experimental import pallas as pl
from jax.experimental.pallas import tpu as pltpu
from jax.sharding import PartitionSpec as P

MESH = pl.DeviceIdType.MESH
CHUNKS = 16
GROUP = 8


def spread_kernel(R, C, S, feat, stored, row_ids, live, buf, deg_x, deg_o, turned, values, fetched, deg_in, ldeg, send_f, recv_f, send_x, recv_x, send_o, recv_o):
    r = lax.axis_index("rows")
    j = lax.axis_index("rep")
    z = r // 2
    y = r % 2
    Z = R // 2
    rows = feat.shape[0] // CHUNKS
    neighbours = ((z < Z - 1, r + 2), (z > 0, r - 2))

    fetch = pltpu.make_async_copy(stored, values, fetched.at[0])
    fetch.start()
    barrier = pltpu.get_barrier_semaphore()
    for d in range(1, C):
        pl.semaphore_signal(barrier, inc=1, device_id=(r, (j + d) % C), device_id_type=MESH)
    pl.semaphore_signal(barrier, inc=1, device_id=(r + 1 - 2 * y, j), device_id_type=MESH)
    for there, target in neighbours:
        @pl.when(there)
        def _():
            pl.semaphore_signal(barrier, inc=1, device_id=(target, j), device_id_type=MESH)
    pl.semaphore_wait(barrier, C + jnp.where(z < Z - 1, 1, 0) + jnp.where(z > 0, 1, 0))

    def feature_copy(s, c, way, target, own):
        place = pl.ds(pl.multiple_of(c * rows, rows), rows)
        dst = buf.at[s, place]
        return pltpu.make_async_remote_copy(
            src_ref=feat.at[place] if own else dst, dst_ref=dst,
            send_sem=send_f.at[s, c, way], recv_sem=recv_f.at[s, c],
            device_id=(target, j), device_id_type=MESH)

    def degree_copy(s, way, target):
        return pltpu.make_async_remote_copy(
            src_ref=deg_x.at[s], dst_ref=deg_x.at[s], send_sem=send_x.at[s, way], recv_sem=recv_x.at[s],
            device_id=(target, j), device_id_type=MESH)

    def ways(s):
        k = s * C + j
        zs = k // 2
        on_column = y == k % 2
        return (
            (0, jnp.logical_and(on_column, jnp.logical_and(z >= zs, z < Z - 1)), r + 2),
            (1, jnp.logical_and(on_column, jnp.logical_and(z <= zs, z > 0)), r - 2),
            (2, on_column, r + 1 - 2 * y),
        )

    def each_chunk(body):
        def step(c, carry):
            body(c)
            return carry
        lax.fori_loop(0, CHUNKS, step, 0)

    for s in range(S):
        @pl.when(r == s * C + j)
        def _():
            def send_chunk(c):
                for way, active, target in ways(s):
                    @pl.when(active)
                    def _():
                        feature_copy(s, c, way, target, True).start()
            each_chunk(send_chunk)

    tile, _, slots = values.shape
    half = tile // 2
    fetch.wait()
    sums = jnp.sum(values[...].astype(jnp.float32), axis=1)
    shape = (ldeg.shape[0], slots)
    row = lax.broadcasted_iota(jnp.int32, shape, 0)
    slot = lax.broadcasted_iota(jnp.int32, shape, 1)
    place = jnp.where(jnp.logical_and(row_ids[...] == row, slot < live[...]), 1.0, 0.0)
    ldeg[...] = lax.dot_general(
        place, sums, (((1,), (1,)), ((), ())),
        precision=lax.Precision.HIGHEST, preferred_element_type=jnp.float32)

    for d in range(1, C):
        pltpu.make_async_remote_copy(
            src_ref=ldeg, dst_ref=deg_in.at[j], send_sem=send_o.at[d], recv_sem=recv_o.at[j],
            device_id=(r, (j + d) % C), device_id_type=MESH).start()

    deg_in[j] = ldeg[...]
    for d in range(1, C):
        a = (j + d) % C
        pltpu.make_async_remote_copy(
            src_ref=ldeg, dst_ref=deg_in.at[a], send_sem=send_o.at[d], recv_sem=recv_o.at[a],
            device_id=(r, a), device_id_type=MESH).wait_recv()
    degree = deg_in[0]
    for a in range(1, C):
        degree = degree + deg_in[a]
    deg_o[...] = degree

    for s in range(S):
        @pl.when(r == s * C + j)
        def _():
            deg_x[s] = degree
            for way, active, target in ways(s):
                @pl.when(active)
                def _():
                    degree_copy(s, way, target).start()
            keep = pltpu.make_async_copy(feat, buf.at[s], fetched.at[1])
            keep.start()
            keep.wait()

    per = -(-half // (S * CHUNKS))

    def turn(step):
        for u in range(per):
            a = step * per + u

            @pl.when(a < half)
            def _():
                pair = jnp.concatenate([values[a], values[a + half]], axis=0).astype(jnp.float32)
                turned[pl.ds(a, slots, stride=half), :] = pair.T

    gaps = [jnp.abs(z - (s * C + j) // 2) for s in range(S)]
    ranks = []
    for s in range(S):
        rank = 0
        for t in range(S):
            if t != s:
                ahead = gaps[t] <= gaps[s] if t < s else gaps[t] < gaps[s]
                rank = rank + jnp.where(ahead, 1, 0)
        ranks.append(rank)
    for i in range(S):
        for s in range(S):
            @pl.when(jnp.logical_and(ranks[s] == i, r == s * C + j))
            def _():
                each_chunk(lambda c: turn(i * CHUNKS + c))

            @pl.when(jnp.logical_and(ranks[s] == i, r != s * C + j))
            def _():
                def pass_chunk(c):
                    turn(i * CHUNKS + c)
                    feature_copy(s, c, 0, r + 1 - 2 * y, False).wait_recv()
                    for way, active, target in ways(s):
                        @pl.when(active)
                        def _():
                            feature_copy(s, c, way, target, False).start()
                each_chunk(pass_chunk)
                degree_copy(s, 0, r + 1 - 2 * y).wait_recv()
                for way, active, target in ways(s):
                    @pl.when(active)
                    def _():
                        degree_copy(s, way, target).start()

    for d in range(1, C):
        pltpu.make_async_remote_copy(
            src_ref=ldeg, dst_ref=deg_in.at[j], send_sem=send_o.at[d], recv_sem=recv_o.at[j],
            device_id=(r, (j + d) % C), device_id_type=MESH).wait_send()
    for s in range(S):
        for way, active, target in ways(s):
            @pl.when(active)
            def _():
                each_chunk(lambda c: feature_copy(s, c, way, target, False).wait_send())
                degree_copy(s, way, target).wait_send()


def tile_kernel(C, tiles, tile, row_ids, columns, count, values, raw, degree, out, total, buf):
    total[...] = jnp.zeros_like(total)
    live = count[0, 0]
    half = tile // 2
    sections = raw.shape[0]
    for s in range(sections):
        inv = lax.rsqrt(1.0 + degree[s].T)
        for a in range(tiles):
            block = raw[s, a * tile:(a + 1) * tile].astype(jnp.float32) * inv[:, a:a + 1]
            start = (s * tiles + a) * tile
            buf[start:start + tile] = block.astype(buf.dtype)

    def group(number, carry):
        products = []
        for u in range(GROUP):
            t = number * GROUP + u
            column = columns[0, t]
            block_index = lax.div(lax.div(column, tiles), C) * tiles + lax.rem(column, tiles)
            start = pl.multiple_of(block_index * tile, tile)
            pair = values[pl.ds(pl.multiple_of(t * half, half), half)]
            block = jnp.concatenate([pair[:, :tile], pair[:, tile:]], axis=0).astype(jnp.bfloat16)
            products.append(
                jnp.dot(block, buf[pl.ds(start, tile)], preferred_element_type=jnp.float32))
        for u in range(GROUP):
            t = number * GROUP + u
            row = jnp.where(t < live, row_ids[0, t], tiles)
            place = pl.ds(pl.multiple_of(row * tile, tile), tile)
            total[place] = total[place] + products[u]
        return carry

    lax.fori_loop(0, (live + GROUP - 1) // GROUP, group, 0)
    out[...] = total[: tiles * tile].astype(out.dtype)


def dense_kernel(R, C, part, features, degree, grad_out, weight, bias, hidden, grad_w, grad_b,
                 arrived, g1, g1_in, g2_in, low,
                 send_p, recv_p, send_h, recv_h, send_1, recv_1, send_2, recv_2, send_w, recv_w):
    r = lax.axis_index("rows")
    j = lax.axis_index("rep")
    barrier = pltpu.get_barrier_semaphore()
    for d in range(1, C):
        pl.semaphore_signal(barrier, inc=1, device_id=(r, (j + d) % C), device_id_type=MESH)
    for d in range(1, R):
        pl.semaphore_signal(barrier, inc=1, device_id=((r + d) % R, j), device_id_type=MESH)
    pl.semaphore_wait(barrier, R + C - 2)

    def to_rep(d, src, dst, send, recv):
        return pltpu.make_async_remote_copy(
            src_ref=src, dst_ref=dst.at[j], send_sem=send.at[d], recv_sem=recv.at[j],
            device_id=(r, (j + d) % C), device_id_type=MESH)

    def from_rep(d, dst, send, recv):
        a = (j + d) % C
        return pltpu.make_async_remote_copy(
            src_ref=dst.at[a], dst_ref=dst.at[a], send_sem=send.at[d], recv_sem=recv.at[a],
            device_id=(r, a), device_id_type=MESH)

    for d in range(1, C):
        to_rep(d, part.at[(j + d) % C], arrived, send_p, recv_p).start()
    q, feat_len = part.shape[1:]
    tile = degree.shape[1]
    mine_rows = pl.ds(pl.multiple_of(j * q, q), q)
    roots = lax.rsqrt(1.0 + degree[...].T)
    lane = lax.broadcasted_iota(jnp.int32, roots.shape, 1)
    inv = jnp.concatenate([
        jnp.broadcast_to(
            jnp.sum(jnp.where(lane == j * (q // tile) + a, roots, 0.0), axis=1, keepdims=True), (tile, feat_len))
        for a in range(q // tile)], axis=0)
    scaled = (features[mine_rows].astype(jnp.float32) * inv).astype(jnp.bfloat16)
    summed = part[j].astype(jnp.float32) + scaled.astype(jnp.float32)
    for d in range(1, C):
        from_rep(d, arrived, send_p, recv_p).wait_recv()
        summed = summed + arrived[(j + d) % C].astype(jnp.float32)
    smoothed = (inv * summed).astype(jnp.bfloat16)
    preact = jnp.dot(smoothed, weight[...], preferred_element_type=jnp.float32) + bias[...]
    sig = 1.0 / (1.0 + jnp.exp(-preact))
    hidden[j] = (preact * sig).astype(jnp.bfloat16)
    grad_pre = grad_out[mine_rows].astype(jnp.float32) * (sig * (1.0 + preact * (1.0 - sig)))
    gb = jnp.sum(grad_pre, axis=0, keepdims=True)
    gw = lax.dot_general(smoothed, grad_pre.astype(jnp.bfloat16), (((0,), (0,)), ((), ())),
                         preferred_element_type=jnp.float32)
    share = gw.shape[0] // C
    for a in range(C):
        g1[a, :share] = gw[a * share:(a + 1) * share]
        g1[a, share:] = jnp.broadcast_to(gb, (8, gb.shape[1]))
    for d in range(1, C):
        to_rep(d, g1.at[(j + d) % C], g1_in, send_1, recv_1).start()
    for d in range(1, C):
        to_rep(d, hidden.at[j], hidden, send_h, recv_h).start()
    g1_in[j] = g1[j]
    for d in range(1, C):
        from_rep(d, g1_in, send_1, recv_1).wait_recv()
    mine = g1_in[0]
    for a in range(1, C):
        mine = mine + g1_in[a]
    low[...] = mine

    def to_rows(d):
        return pltpu.make_async_remote_copy(
            src_ref=low, dst_ref=g2_in.at[r], send_sem=send_2.at[d], recv_sem=recv_2.at[r],
            device_id=((r + d) % R, j), device_id_type=MESH)

    for d in range(1, R):
        to_rows(d).start()
    g2_in[r] = mine
    for d in range(1, R):
        a = (r + d) % R
        pltpu.make_async_remote_copy(
            src_ref=low, dst_ref=g2_in.at[a], send_sem=send_2.at[d], recv_sem=recv_2.at[a],
            device_id=(a, j), device_id_type=MESH).wait_recv()
    whole = g2_in[0]
    for a in range(1, R):
        whole = whole + g2_in[a]
    grad_w[j] = whole[:share]
    grad_b[...] = whole[share:share + 1]
    for d in range(1, C):
        to_rep(d, grad_w.at[j], grad_w, send_w, recv_w).start()
    for d in range(1, C):
        from_rep(d, grad_w, send_w, recv_w).wait_recv()
        from_rep(d, hidden, send_h, recv_h).wait_recv()
    for d in range(1, C):
        to_rep(d, part.at[(j + d) % C], arrived, send_p, recv_p).wait_send()
        to_rep(d, hidden.at[j], hidden, send_h, recv_h).wait_send()
        to_rep(d, g1.at[(j + d) % C], g1_in, send_1, recv_1).wait_send()
        to_rep(d, grad_w.at[j], grad_w, send_w, recv_w).wait_send()
    for d in range(1, R):
        to_rows(d).wait_send()


def local(features, weight, bias, grad_out, tile_values, tile_rows, tile_cols, tile_count):
    values = tile_values[0, 0]
    N, F = features.shape
    T, tile = values.shape[0], values.shape[1]
    tiles = N // tile
    R = lax.axis_size("rows")
    C = lax.axis_size("rep")
    S = R // C
    vmem = pl.BlockSpec(memory_space=pltpu.VMEM)
    anywhere = pl.BlockSpec(memory_space=pltpu.HBM)
    smem = pl.BlockSpec(memory_space=pltpu.SMEM)
    dma = pltpu.SemaphoreType.DMA
    f32, bf16 = jnp.float32, jnp.bfloat16
    sds = jax.ShapeDtypeStruct

    buf, deg_x, deg_o, turned = pl.pallas_call(
        functools.partial(spread_kernel, R, C, S),
        out_shape=(sds((S, N, F), bf16), sds((S, tiles, tile), f32), sds((tiles, tile), f32),
                   sds((T * tile // 2, 2 * tile), f32)),
        in_specs=[anywhere, anywhere, vmem, vmem],
        out_specs=(vmem,) * 4,
        scratch_shapes=[
            pltpu.VMEM((tile, tile, T), bf16), dma((2,)),
            pltpu.VMEM((C, tiles, tile), f32), pltpu.VMEM((tiles, tile), f32),
            dma((S, CHUNKS, 3)), dma((S, CHUNKS)), dma((S, 3)), dma((S,)), dma((C,)), dma((C,))],
        compiler_params=pltpu.CompilerParams(
            collective_id=0, has_side_effects=True, vmem_limit_bytes=32 * 2**20),
    )(features, jnp.transpose(values, (1, 2, 0)), tile_rows[0], tile_count)

    part = pl.pallas_call(
        functools.partial(tile_kernel, C, tiles, tile),
        out_shape=sds((N, F), bf16),
        in_specs=[smem, smem, smem, vmem, vmem, vmem],
        out_specs=vmem,
        scratch_shapes=[pltpu.VMEM(((tiles + 1) * tile, F), f32), pltpu.VMEM((S * N, F), bf16)],
        compiler_params=pltpu.CompilerParams(vmem_limit_bytes=32 * 2**20),
    )(tile_rows[0], tile_cols[0], tile_count, turned, buf, deg_x)

    q = N // C
    share = F // C
    hidden, grad_w, grad_b = pl.pallas_call(
        functools.partial(dense_kernel, R, C),
        out_shape=(sds((C, q, F), bf16), sds((C, share, F), f32), sds((1, F), f32)),
        in_specs=[vmem] * 6,
        out_specs=(vmem,) * 3,
        scratch_shapes=[
            pltpu.VMEM((C, q, F), bf16),
            pltpu.VMEM((C, share + 8, F), f32),
            pltpu.VMEM((C, share + 8, F), f32),
            pltpu.VMEM((R, share + 8, F), f32),
            pltpu.VMEM((share + 8, F), f32),
            dma((C,)), dma((C,)), dma((C,)), dma((C,)), dma((C,)), dma((C,)), dma((R,)), dma((R,)),
            dma((C,)), dma((C,))],
        compiler_params=pltpu.CompilerParams(
            collective_id=1, has_side_effects=True, vmem_limit_bytes=32 * 2**20),
    )(part.reshape(C, q, F), features, deg_o, grad_out, weight, bias[None, :])
    return (hidden.reshape(N, F), grad_w.reshape(F, F), grad_b.reshape(F))


def solution(mesh):
    return jax.shard_map(
        local,
        mesh=mesh,
        in_specs=(
            P("rows", None),
            P(),
            P(),
            P("rows", None),
            P("rows", "rep", None, None, None),
            P("rows", "rep", None),
            P("rows", "rep", None),
            P("rows", "rep"),
        ),
        out_specs=(P("rows", None), P(), P()),
        check_vma=False,
    )
```

```python
import functools
import jax
import jax.numpy as jnp
from jax import lax
from jax.experimental import pallas as pl
from jax.experimental.pallas import tpu as pltpu
from jax.sharding import PartitionSpec as P

MESH = pl.DeviceIdType.MESH
CHUNKS = 16
GROUP = 8
PARTS = 4


def spread_kernel(R, C, S, feat, stored, row_ids, live, buf, deg_x, deg_o, turned, values, fetched, deg_in, ldeg, send_f, recv_f, send_x, recv_x, send_o, recv_o):
    r = lax.axis_index("rows")
    j = lax.axis_index("rep")
    z = r // 2
    y = r % 2
    Z = R // 2
    rows = feat.shape[0] // CHUNKS
    neighbours = ((z < Z - 1, r + 2), (z > 0, r - 2))

    fetch = pltpu.make_async_copy(stored, values, fetched.at[0])
    fetch.start()
    barrier = pltpu.get_barrier_semaphore()
    for d in range(1, C):
        pl.semaphore_signal(barrier, inc=1, device_id=(r, (j + d) % C), device_id_type=MESH)
    pl.semaphore_signal(barrier, inc=1, device_id=(r + 1 - 2 * y, j), device_id_type=MESH)
    for there, target in neighbours:
        @pl.when(there)
        def _():
            pl.semaphore_signal(barrier, inc=1, device_id=(target, j), device_id_type=MESH)
    pl.semaphore_wait(barrier, C + jnp.where(z < Z - 1, 1, 0) + jnp.where(z > 0, 1, 0))

    def feature_copy(s, c, way, target, own):
        place = pl.ds(pl.multiple_of(c * rows, rows), rows)
        dst = buf.at[s, place]
        return pltpu.make_async_remote_copy(
            src_ref=feat.at[place] if own else dst, dst_ref=dst,
            send_sem=send_f.at[s, c, way], recv_sem=recv_f.at[s, c],
            device_id=(target, j), device_id_type=MESH)

    def degree_copy(s, way, target):
        return pltpu.make_async_remote_copy(
            src_ref=deg_x.at[s], dst_ref=deg_x.at[s], send_sem=send_x.at[s, way], recv_sem=recv_x.at[s],
            device_id=(target, j), device_id_type=MESH)

    def ways(s):
        k = s * C + j
        zs = k // 2
        on_column = y == k % 2
        return (
            (0, jnp.logical_and(on_column, jnp.logical_and(z >= zs, z < Z - 1)), r + 2),
            (1, jnp.logical_and(on_column, jnp.logical_and(z <= zs, z > 0)), r - 2),
            (2, on_column, r + 1 - 2 * y),
        )

    def each_chunk(body):
        def step(c, carry):
            body(c)
            return carry
        lax.fori_loop(0, CHUNKS, step, 0)

    for s in range(S):
        @pl.when(r == s * C + j)
        def _():
            def send_chunk(c):
                for way, active, target in ways(s):
                    @pl.when(active)
                    def _():
                        feature_copy(s, c, way, target, True).start()
            each_chunk(send_chunk)

    tile, _, slots = values.shape
    half = tile // 2
    fetch.wait()
    sums = jnp.sum(values[...].astype(jnp.float32), axis=1)
    shape = (ldeg.shape[0], slots)
    row = lax.broadcasted_iota(jnp.int32, shape, 0)
    slot = lax.broadcasted_iota(jnp.int32, shape, 1)
    place = jnp.where(jnp.logical_and(row_ids[...] == row, slot < live[...]), 1.0, 0.0)
    ldeg[...] = lax.dot_general(
        place, sums, (((1,), (1,)), ((), ())),
        precision=lax.Precision.HIGHEST, preferred_element_type=jnp.float32)

    for d in range(1, C):
        pltpu.make_async_remote_copy(
            src_ref=ldeg, dst_ref=deg_in.at[j], send_sem=send_o.at[d], recv_sem=recv_o.at[j],
            device_id=(r, (j + d) % C), device_id_type=MESH).start()

    deg_in[j] = ldeg[...]
    for d in range(1, C):
        a = (j + d) % C
        pltpu.make_async_remote_copy(
            src_ref=ldeg, dst_ref=deg_in.at[a], send_sem=send_o.at[d], recv_sem=recv_o.at[a],
            device_id=(r, a), device_id_type=MESH).wait_recv()
    degree = deg_in[0]
    for a in range(1, C):
        degree = degree + deg_in[a]
    deg_o[...] = degree

    for s in range(S):
        @pl.when(r == s * C + j)
        def _():
            deg_x[s] = degree
            for way, active, target in ways(s):
                @pl.when(active)
                def _():
                    degree_copy(s, way, target).start()
            keep = pltpu.make_async_copy(feat, buf.at[s], fetched.at[1])
            keep.start()
            keep.wait()

    per = -(-half // (S * CHUNKS))

    def turn(step):
        for u in range(per):
            a = step * per + u

            @pl.when(a < half)
            def _():
                pair = jnp.concatenate([values[a], values[a + half]], axis=0).astype(jnp.float32)
                turned[pl.ds(a, slots, stride=half), :] = pair.T

    gaps = [jnp.abs(z - (s * C + j) // 2) for s in range(S)]
    ranks = []
    for s in range(S):
        rank = 0
        for t in range(S):
            if t != s:
                ahead = gaps[t] <= gaps[s] if t < s else gaps[t] < gaps[s]
                rank = rank + jnp.where(ahead, 1, 0)
        ranks.append(rank)
    for i in range(S):
        for s in range(S):
            @pl.when(jnp.logical_and(ranks[s] == i, r == s * C + j))
            def _():
                each_chunk(lambda c: turn(i * CHUNKS + c))

            @pl.when(jnp.logical_and(ranks[s] == i, r != s * C + j))
            def _():
                def pass_chunk(c):
                    turn(i * CHUNKS + c)
                    feature_copy(s, c, 0, r + 1 - 2 * y, False).wait_recv()
                    for way, active, target in ways(s):
                        @pl.when(active)
                        def _():
                            feature_copy(s, c, way, target, False).start()
                each_chunk(pass_chunk)
                degree_copy(s, 0, r + 1 - 2 * y).wait_recv()
                for way, active, target in ways(s):
                    @pl.when(active)
                    def _():
                        degree_copy(s, way, target).start()

    for d in range(1, C):
        pltpu.make_async_remote_copy(
            src_ref=ldeg, dst_ref=deg_in.at[j], send_sem=send_o.at[d], recv_sem=recv_o.at[j],
            device_id=(r, (j + d) % C), device_id_type=MESH).wait_send()
    for s in range(S):
        for way, active, target in ways(s):
            @pl.when(active)
            def _():
                each_chunk(lambda c: feature_copy(s, c, way, target, False).wait_send())
                degree_copy(s, way, target).wait_send()


def tile_kernel(C, tiles, tile, row_ids, columns, count, values, raw, degree, out, total, buf):
    total[...] = jnp.zeros_like(total)
    live = count[0, 0]
    half = tile // 2
    sections = raw.shape[0]
    for s in range(sections):
        inv = lax.rsqrt(1.0 + degree[s].T)
        for a in range(tiles):
            block = raw[s, a * tile:(a + 1) * tile].astype(jnp.float32) * inv[:, a:a + 1]
            start = (s * tiles + a) * tile
            buf[start:start + tile] = block.astype(buf.dtype)

    def group(number, carry):
        products = []
        for u in range(GROUP):
            t = number * GROUP + u
            column = columns[0, t]
            block_index = lax.div(lax.div(column, tiles), C) * tiles + lax.rem(column, tiles)
            start = pl.multiple_of(block_index * tile, tile)
            pair = values[pl.ds(pl.multiple_of(t * half, half), half)]
            block = jnp.concatenate([pair[:, :tile], pair[:, tile:]], axis=0).astype(jnp.bfloat16)
            products.append(
                jnp.dot(block, buf[pl.ds(start, tile)], preferred_element_type=jnp.float32))
        for u in range(GROUP):
            t = number * GROUP + u
            row = jnp.where(t < live, row_ids[0, t], tiles)
            place = pl.ds(pl.multiple_of(row * tile, tile), tile)
            total[place] = total[place] + products[u]
        return carry

    lax.fori_loop(0, (live + GROUP - 1) // GROUP, group, 0)
    out[...] = total[: tiles * tile].astype(out.dtype)


def dense_kernel(R, C, part, features, degree, grad_out, weight, bias, hidden, grad_w, grad_b,
                 arrived, g1, g1_in, g2_in, low,
                 send_p, recv_p, send_h, recv_h, send_1, recv_1, send_2, recv_2, send_w, recv_w):
    r = lax.axis_index("rows")
    j = lax.axis_index("rep")
    barrier = pltpu.get_barrier_semaphore()
    for d in range(1, C):
        pl.semaphore_signal(barrier, inc=1, device_id=(r, (j + d) % C), device_id_type=MESH)
    for d in range(1, R):
        pl.semaphore_signal(barrier, inc=1, device_id=((r + d) % R, j), device_id_type=MESH)
    pl.semaphore_wait(barrier, R + C - 2)

    def to_rep(d, src, dst, send, recv):
        return pltpu.make_async_remote_copy(
            src_ref=src, dst_ref=dst.at[j], send_sem=send.at[d], recv_sem=recv.at[j],
            device_id=(r, (j + d) % C), device_id_type=MESH)

    def from_rep(d, dst, send, recv):
        a = (j + d) % C
        return pltpu.make_async_remote_copy(
            src_ref=dst.at[a], dst_ref=dst.at[a], send_sem=send.at[d], recv_sem=recv.at[a],
            device_id=(r, a), device_id_type=MESH)

    q, feat_len = part.shape[1:]
    step = q // PARTS

    def to_owner(d, h):
        rows = pl.ds(h * step, step)
        return pltpu.make_async_remote_copy(
            src_ref=part.at[(j + d) % C, rows], dst_ref=arrived.at[j, rows],
            send_sem=send_p.at[d, h], recv_sem=recv_p.at[j, h],
            device_id=(r, (j + d) % C), device_id_type=MESH)

    for h in range(PARTS):
        for d in range(1, C):
            to_owner(d, h).start()
    tile = degree.shape[1]
    roots = lax.rsqrt(1.0 + degree[...].T)
    lane = lax.broadcasted_iota(jnp.int32, roots.shape, 1)
    inv_all = jnp.concatenate([
        jnp.broadcast_to(
            jnp.sum(jnp.where(lane == j * (q // tile) + a, roots, 0.0), axis=1, keepdims=True), (tile, feat_len))
        for a in range(q // tile)], axis=0)
    gb = jnp.zeros((1, feat_len), jnp.float32)
    gw = jnp.zeros((feat_len, feat_len), jnp.float32)
    for h in range(PARTS):
        rows = slice(h * step, (h + 1) * step)
        whole_rows = pl.ds(pl.multiple_of(j * q + h * step, step), step)
        inv = inv_all[rows]
        scaled = (features[whole_rows].astype(jnp.float32) * inv).astype(jnp.bfloat16)
        summed = part[j, rows].astype(jnp.float32) + scaled.astype(jnp.float32)
        for d in range(1, C):
            a = (j + d) % C
            place = pl.ds(h * step, step)
            pltpu.make_async_remote_copy(
                src_ref=arrived.at[a, place], dst_ref=arrived.at[a, place],
                send_sem=send_p.at[d, h], recv_sem=recv_p.at[a, h],
                device_id=(r, a), device_id_type=MESH).wait_recv()
            summed = summed + arrived[a, rows].astype(jnp.float32)
        smoothed = (inv * summed).astype(jnp.bfloat16)
        preact = jnp.dot(smoothed, weight[...], preferred_element_type=jnp.float32) + bias[...]
        sig = 1.0 / (1.0 + jnp.exp(-preact))
        hidden[j, rows] = (preact * sig).astype(jnp.bfloat16)
        grad_pre = grad_out[whole_rows].astype(jnp.float32) * (sig * (1.0 + preact * (1.0 - sig)))
        gb = gb + jnp.sum(grad_pre, axis=0, keepdims=True)
        gw = gw + lax.dot_general(
            smoothed, grad_pre.astype(jnp.bfloat16), (((0,), (0,)), ((), ())),
            preferred_element_type=jnp.float32)
    share = gw.shape[0] // C
    for a in range(C):
        g1[a, :share] = gw[a * share:(a + 1) * share]
        g1[a, share:] = jnp.broadcast_to(gb, (8, gb.shape[1]))
    for d in range(1, C):
        to_rep(d, g1.at[(j + d) % C], g1_in, send_1, recv_1).start()
    for d in range(1, C):
        to_rep(d, hidden.at[j], hidden, send_h, recv_h).start()
    g1_in[j] = g1[j]
    for d in range(1, C):
        from_rep(d, g1_in, send_1, recv_1).wait_recv()
    mine = g1_in[0]
    for a in range(1, C):
        mine = mine + g1_in[a]
    low[...] = mine

    def to_rows(d):
        return pltpu.make_async_remote_copy(
            src_ref=low, dst_ref=g2_in.at[r], send_sem=send_2.at[d], recv_sem=recv_2.at[r],
            device_id=((r + d) % R, j), device_id_type=MESH)

    for d in range(1, R):
        to_rows(d).start()
    g2_in[r] = mine
    for d in range(1, R):
        a = (r + d) % R
        pltpu.make_async_remote_copy(
            src_ref=low, dst_ref=g2_in.at[a], send_sem=send_2.at[d], recv_sem=recv_2.at[a],
            device_id=(a, j), device_id_type=MESH).wait_recv()
    whole = g2_in[0]
    for a in range(1, R):
        whole = whole + g2_in[a]
    grad_w[j] = whole[:share]
    grad_b[...] = whole[share:share + 1]
    for d in range(1, C):
        to_rep(d, grad_w.at[j], grad_w, send_w, recv_w).start()
    for d in range(1, C):
        from_rep(d, grad_w, send_w, recv_w).wait_recv()
        from_rep(d, hidden, send_h, recv_h).wait_recv()
    for d in range(1, C):
        for h in range(PARTS):
            to_owner(d, h).wait_send()
        to_rep(d, hidden.at[j], hidden, send_h, recv_h).wait_send()
        to_rep(d, g1.at[(j + d) % C], g1_in, send_1, recv_1).wait_send()
        to_rep(d, grad_w.at[j], grad_w, send_w, recv_w).wait_send()
    for d in range(1, R):
        to_rows(d).wait_send()


def local(features, weight, bias, grad_out, tile_values, tile_rows, tile_cols, tile_count):
    values = tile_values[0, 0]
    N, F = features.shape
    T, tile = values.shape[0], values.shape[1]
    tiles = N // tile
    R = lax.axis_size("rows")
    C = lax.axis_size("rep")
    S = R // C
    vmem = pl.BlockSpec(memory_space=pltpu.VMEM)
    anywhere = pl.BlockSpec(memory_space=pltpu.HBM)
    smem = pl.BlockSpec(memory_space=pltpu.SMEM)
    dma = pltpu.SemaphoreType.DMA
    f32, bf16 = jnp.float32, jnp.bfloat16
    sds = jax.ShapeDtypeStruct

    buf, deg_x, deg_o, turned = pl.pallas_call(
        functools.partial(spread_kernel, R, C, S),
        out_shape=(sds((S, N, F), bf16), sds((S, tiles, tile), f32), sds((tiles, tile), f32),
                   sds((T * tile // 2, 2 * tile), f32)),
        in_specs=[anywhere, anywhere, vmem, vmem],
        out_specs=(vmem,) * 4,
        scratch_shapes=[
            pltpu.VMEM((tile, tile, T), bf16), dma((2,)),
            pltpu.VMEM((C, tiles, tile), f32), pltpu.VMEM((tiles, tile), f32),
            dma((S, CHUNKS, 3)), dma((S, CHUNKS)), dma((S, 3)), dma((S,)), dma((C,)), dma((C,))],
        compiler_params=pltpu.CompilerParams(
            collective_id=0, has_side_effects=True, vmem_limit_bytes=32 * 2**20),
    )(features, jnp.transpose(values, (1, 2, 0)), tile_rows[0], tile_count)

    part = pl.pallas_call(
        functools.partial(tile_kernel, C, tiles, tile),
        out_shape=sds((N, F), bf16),
        in_specs=[smem, smem, smem, vmem, vmem, vmem],
        out_specs=vmem,
        scratch_shapes=[pltpu.VMEM(((tiles + 1) * tile, F), f32), pltpu.VMEM((S * N, F), bf16)],
        compiler_params=pltpu.CompilerParams(vmem_limit_bytes=32 * 2**20),
    )(tile_rows[0], tile_cols[0], tile_count, turned, buf, deg_x)

    q = N // C
    share = F // C
    hidden, grad_w, grad_b = pl.pallas_call(
        functools.partial(dense_kernel, R, C),
        out_shape=(sds((C, q, F), bf16), sds((C, share, F), f32), sds((1, F), f32)),
        in_specs=[vmem] * 6,
        out_specs=(vmem,) * 3,
        scratch_shapes=[
            pltpu.VMEM((C, q, F), bf16),
            pltpu.VMEM((C, share + 8, F), f32),
            pltpu.VMEM((C, share + 8, F), f32),
            pltpu.VMEM((R, share + 8, F), f32),
            pltpu.VMEM((share + 8, F), f32),
            dma((C, PARTS)), dma((C, PARTS)), dma((C,)), dma((C,)), dma((C,)), dma((C,)), dma((R,)), dma((R,)),
            dma((C,)), dma((C,))],
        compiler_params=pltpu.CompilerParams(
            collective_id=1, has_side_effects=True, vmem_limit_bytes=32 * 2**20),
    )(part.reshape(C, q, F), features, deg_o, grad_out, weight, bias[None, :])
    return (hidden.reshape(N, F), grad_w.reshape(F, F), grad_b.reshape(F))


def solution(mesh):
    return jax.shard_map(
        local,
        mesh=mesh,
        in_specs=(
            P("rows", None),
            P(),
            P(),
            P("rows", None),
            P("rows", "rep", None, None, None),
            P("rows", "rep", None),
            P("rows", "rep", None),
            P("rows", "rep"),
        ),
        out_specs=(P("rows", None), P(), P()),
        check_vma=False,
    )
```

```python
import functools
import jax
import jax.numpy as jnp
from jax import lax
from jax.experimental import pallas as pl
from jax.experimental.pallas import tpu as pltpu
from jax.sharding import PartitionSpec as P

MESH = pl.DeviceIdType.MESH
CHUNKS = 16
GROUP = 32
PARTS = 4


def spread_kernel(R, C, S, feat, stored, row_ids, live, buf, deg_x, deg_o, turned, values, fetched, deg_in, ldeg, send_f, recv_f, send_x, recv_x, send_o, recv_o):
    r = lax.axis_index("rows")
    j = lax.axis_index("rep")
    z = r // 2
    y = r % 2
    Z = R // 2
    rows = feat.shape[0] // CHUNKS
    neighbours = ((z < Z - 1, r + 2), (z > 0, r - 2))

    fetch = pltpu.make_async_copy(stored, values, fetched.at[0])
    fetch.start()
    barrier = pltpu.get_barrier_semaphore()
    for d in range(1, C):
        pl.semaphore_signal(barrier, inc=1, device_id=(r, (j + d) % C), device_id_type=MESH)
    pl.semaphore_signal(barrier, inc=1, device_id=(r + 1 - 2 * y, j), device_id_type=MESH)
    for there, target in neighbours:
        @pl.when(there)
        def _():
            pl.semaphore_signal(barrier, inc=1, device_id=(target, j), device_id_type=MESH)
    pl.semaphore_wait(barrier, C + jnp.where(z < Z - 1, 1, 0) + jnp.where(z > 0, 1, 0))

    def feature_copy(s, c, way, target, own):
        place = pl.ds(pl.multiple_of(c * rows, rows), rows)
        dst = buf.at[s, place]
        return pltpu.make_async_remote_copy(
            src_ref=feat.at[place] if own else dst, dst_ref=dst,
            send_sem=send_f.at[s, c, way], recv_sem=recv_f.at[s, c],
            device_id=(target, j), device_id_type=MESH)

    def degree_copy(s, way, target):
        return pltpu.make_async_remote_copy(
            src_ref=deg_x.at[s], dst_ref=deg_x.at[s], send_sem=send_x.at[s, way], recv_sem=recv_x.at[s],
            device_id=(target, j), device_id_type=MESH)

    def ways(s):
        k = s * C + j
        zs = k // 2
        on_column = y == k % 2
        return (
            (0, jnp.logical_and(on_column, jnp.logical_and(z >= zs, z < Z - 1)), r + 2),
            (1, jnp.logical_and(on_column, jnp.logical_and(z <= zs, z > 0)), r - 2),
            (2, on_column, r + 1 - 2 * y),
        )

    def each_chunk(body):
        def step(c, carry):
            body(c)
            return carry
        lax.fori_loop(0, CHUNKS, step, 0)

    for s in range(S):
        @pl.when(r == s * C + j)
        def _():
            def send_chunk(c):
                for way, active, target in ways(s):
                    @pl.when(active)
                    def _():
                        feature_copy(s, c, way, target, True).start()
            each_chunk(send_chunk)

    tile, _, slots = values.shape
    half = tile // 2
    fetch.wait()
    sums = jnp.sum(values[...].astype(jnp.float32), axis=1)
    shape = (ldeg.shape[0], slots)
    row = lax.broadcasted_iota(jnp.int32, shape, 0)
    slot = lax.broadcasted_iota(jnp.int32, shape, 1)
    place = jnp.where(jnp.logical_and(row_ids[...] == row, slot < live[...]), 1.0, 0.0)
    ldeg[...] = lax.dot_general(
        place, sums, (((1,), (1,)), ((), ())),
        precision=lax.Precision.HIGHEST, preferred_element_type=jnp.float32)

    for d in range(1, C):
        pltpu.make_async_remote_copy(
            src_ref=ldeg, dst_ref=deg_in.at[j], send_sem=send_o.at[d], recv_sem=recv_o.at[j],
            device_id=(r, (j + d) % C), device_id_type=MESH).start()

    deg_in[j] = ldeg[...]
    for d in range(1, C):
        a = (j + d) % C
        pltpu.make_async_remote_copy(
            src_ref=ldeg, dst_ref=deg_in.at[a], send_sem=send_o.at[d], recv_sem=recv_o.at[a],
            device_id=(r, a), device_id_type=MESH).wait_recv()
    degree = deg_in[0]
    for a in range(1, C):
        degree = degree + deg_in[a]
    deg_o[...] = degree

    for s in range(S):
        @pl.when(r == s * C + j)
        def _():
            deg_x[s] = degree
            for way, active, target in ways(s):
                @pl.when(active)
                def _():
                    degree_copy(s, way, target).start()
            keep = pltpu.make_async_copy(feat, buf.at[s], fetched.at[1])
            keep.start()
            keep.wait()

    per = -(-half // (S * CHUNKS))

    def turn(step):
        for u in range(per):
            a = step * per + u

            @pl.when(a < half)
            def _():
                pair = jnp.concatenate([values[a], values[a + half]], axis=0).astype(jnp.float32)
                turned[pl.ds(a, slots, stride=half), :] = pair.T

    gaps = [jnp.abs(z - (s * C + j) // 2) for s in range(S)]
    ranks = []
    for s in range(S):
        rank = 0
        for t in range(S):
            if t != s:
                ahead = gaps[t] <= gaps[s] if t < s else gaps[t] < gaps[s]
                rank = rank + jnp.where(ahead, 1, 0)
        ranks.append(rank)
    for i in range(S):
        for s in range(S):
            @pl.when(jnp.logical_and(ranks[s] == i, r == s * C + j))
            def _():
                each_chunk(lambda c: turn(i * CHUNKS + c))

            @pl.when(jnp.logical_and(ranks[s] == i, r != s * C + j))
            def _():
                def pass_chunk(c):
                    turn(i * CHUNKS + c)
                    feature_copy(s, c, 0, r + 1 - 2 * y, False).wait_recv()
                    for way, active, target in ways(s):
                        @pl.when(active)
                        def _():
                            feature_copy(s, c, way, target, False).start()
                each_chunk(pass_chunk)
                degree_copy(s, 0, r + 1 - 2 * y).wait_recv()
                for way, active, target in ways(s):
                    @pl.when(active)
                    def _():
                        degree_copy(s, way, target).start()

    for d in range(1, C):
        pltpu.make_async_remote_copy(
            src_ref=ldeg, dst_ref=deg_in.at[j], send_sem=send_o.at[d], recv_sem=recv_o.at[j],
            device_id=(r, (j + d) % C), device_id_type=MESH).wait_send()
    for s in range(S):
        for way, active, target in ways(s):
            @pl.when(active)
            def _():
                each_chunk(lambda c: feature_copy(s, c, way, target, False).wait_send())
                degree_copy(s, way, target).wait_send()


def tile_kernel(C, tiles, tile, row_ids, columns, count, values, raw, degree, out, total, buf):
    total[...] = jnp.zeros_like(total)
    live = count[0, 0]
    half = tile // 2
    sections = raw.shape[0]
    for s in range(sections):
        inv = lax.rsqrt(1.0 + degree[s].T)
        for a in range(tiles):
            block = raw[s, a * tile:(a + 1) * tile].astype(jnp.float32) * inv[:, a:a + 1]
            start = (s * tiles + a) * tile
            buf[start:start + tile] = block.astype(buf.dtype)

    def group(number, carry):
        products = []
        for u in range(GROUP):
            t = number * GROUP + u
            column = columns[0, t]
            block_index = lax.div(lax.div(column, tiles), C) * tiles + lax.rem(column, tiles)
            start = pl.multiple_of(block_index * tile, tile)
            pair = values[pl.ds(pl.multiple_of(t * half, half), half)]
            block = jnp.concatenate([pair[:, :tile], pair[:, tile:]], axis=0).astype(jnp.bfloat16)
            products.append(
                jnp.dot(block, buf[pl.ds(start, tile)], preferred_element_type=jnp.float32))
        for u in range(GROUP):
            t = number * GROUP + u
            row = jnp.where(t < live, row_ids[0, t], tiles)
            place = pl.ds(pl.multiple_of(row * tile, tile), tile)
            total[place] = total[place] + products[u]
        return carry

    lax.fori_loop(0, (live + GROUP - 1) // GROUP, group, 0)
    out[...] = total[: tiles * tile].astype(out.dtype)


def dense_kernel(R, C, part, features, degree, grad_out, weight, bias, hidden, grad_w, grad_b,
                 arrived, g1, g1_in, g2_in, low,
                 send_p, recv_p, send_h, recv_h, send_1, recv_1, send_2, recv_2, send_w, recv_w):
    r = lax.axis_index("rows")
    j = lax.axis_index("rep")
    barrier = pltpu.get_barrier_semaphore()
    for d in range(1, C):
        pl.semaphore_signal(barrier, inc=1, device_id=(r, (j + d) % C), device_id_type=MESH)
    for d in range(1, R):
        pl.semaphore_signal(barrier, inc=1, device_id=((r + d) % R, j), device_id_type=MESH)
    pl.semaphore_wait(barrier, R + C - 2)

    def to_rep(d, src, dst, send, recv):
        return pltpu.make_async_remote_copy(
            src_ref=src, dst_ref=dst.at[j], send_sem=send.at[d], recv_sem=recv.at[j],
            device_id=(r, (j + d) % C), device_id_type=MESH)

    def from_rep(d, dst, send, recv):
        a = (j + d) % C
        return pltpu.make_async_remote_copy(
            src_ref=dst.at[a], dst_ref=dst.at[a], send_sem=send.at[d], recv_sem=recv.at[a],
            device_id=(r, a), device_id_type=MESH)

    q, feat_len = part.shape[1:]
    step = q // PARTS

    def to_owner(d, h):
        rows = pl.ds(h * step, step)
        return pltpu.make_async_remote_copy(
            src_ref=part.at[(j + d) % C, rows], dst_ref=arrived.at[j, rows],
            send_sem=send_p.at[d, h], recv_sem=recv_p.at[j, h],
            device_id=(r, (j + d) % C), device_id_type=MESH)

    for h in range(PARTS):
        for d in range(1, C):
            to_owner(d, h).start()
    tile = degree.shape[1]
    roots = lax.rsqrt(1.0 + degree[...].T)
    lane = lax.broadcasted_iota(jnp.int32, roots.shape, 1)
    inv_all = jnp.concatenate([
        jnp.broadcast_to(
            jnp.sum(jnp.where(lane == j * (q // tile) + a, roots, 0.0), axis=1, keepdims=True), (tile, feat_len))
        for a in range(q // tile)], axis=0)
    gb = jnp.zeros((1, feat_len), jnp.float32)
    gw = jnp.zeros((feat_len, feat_len), jnp.float32)
    for h in range(PARTS):
        rows = slice(h * step, (h + 1) * step)
        whole_rows = pl.ds(pl.multiple_of(j * q + h * step, step), step)
        inv = inv_all[rows]
        scaled = (features[whole_rows].astype(jnp.float32) * inv).astype(jnp.bfloat16)
        summed = part[j, rows].astype(jnp.float32) + scaled.astype(jnp.float32)
        for d in range(1, C):
            a = (j + d) % C
            place = pl.ds(h * step, step)
            pltpu.make_async_remote_copy(
                src_ref=arrived.at[a, place], dst_ref=arrived.at[a, place],
                send_sem=send_p.at[d, h], recv_sem=recv_p.at[a, h],
                device_id=(r, a), device_id_type=MESH).wait_recv()
            summed = summed + arrived[a, rows].astype(jnp.float32)
        smoothed = (inv * summed).astype(jnp.bfloat16)
        preact = jnp.dot(smoothed, weight[...], preferred_element_type=jnp.float32) + bias[...]
        sig = 1.0 / (1.0 + jnp.exp(-preact))
        hidden[j, rows] = (preact * sig).astype(jnp.bfloat16)
        grad_pre = grad_out[whole_rows].astype(jnp.float32) * (sig * (1.0 + preact * (1.0 - sig)))
        gb = gb + jnp.sum(grad_pre, axis=0, keepdims=True)
        gw = gw + lax.dot_general(
            smoothed, grad_pre.astype(jnp.bfloat16), (((0,), (0,)), ((), ())),
            preferred_element_type=jnp.float32)
    share = gw.shape[0] // C
    for a in range(C):
        g1[a, :share] = gw[a * share:(a + 1) * share]
        g1[a, share:] = jnp.broadcast_to(gb, (8, gb.shape[1]))
    for d in range(1, C):
        to_rep(d, g1.at[(j + d) % C], g1_in, send_1, recv_1).start()
    for d in range(1, C):
        to_rep(d, hidden.at[j], hidden, send_h, recv_h).start()
    g1_in[j] = g1[j]
    for d in range(1, C):
        from_rep(d, g1_in, send_1, recv_1).wait_recv()
    mine = g1_in[0]
    for a in range(1, C):
        mine = mine + g1_in[a]
    low[...] = mine

    def to_rows(d):
        return pltpu.make_async_remote_copy(
            src_ref=low, dst_ref=g2_in.at[r], send_sem=send_2.at[d], recv_sem=recv_2.at[r],
            device_id=((r + d) % R, j), device_id_type=MESH)

    for d in range(1, R):
        to_rows(d).start()
    g2_in[r] = mine
    for d in range(1, R):
        a = (r + d) % R
        pltpu.make_async_remote_copy(
            src_ref=low, dst_ref=g2_in.at[a], send_sem=send_2.at[d], recv_sem=recv_2.at[a],
            device_id=(a, j), device_id_type=MESH).wait_recv()
    whole = g2_in[0]
    for a in range(1, R):
        whole = whole + g2_in[a]
    grad_w[j] = whole[:share]
    grad_b[...] = whole[share:share + 1]
    for d in range(1, C):
        to_rep(d, grad_w.at[j], grad_w, send_w, recv_w).start()
    for d in range(1, C):
        from_rep(d, grad_w, send_w, recv_w).wait_recv()
        from_rep(d, hidden, send_h, recv_h).wait_recv()
    for d in range(1, C):
        for h in range(PARTS):
            to_owner(d, h).wait_send()
        to_rep(d, hidden.at[j], hidden, send_h, recv_h).wait_send()
        to_rep(d, g1.at[(j + d) % C], g1_in, send_1, recv_1).wait_send()
        to_rep(d, grad_w.at[j], grad_w, send_w, recv_w).wait_send()
    for d in range(1, R):
        to_rows(d).wait_send()


def local(features, weight, bias, grad_out, tile_values, tile_rows, tile_cols, tile_count):
    values = tile_values[0, 0]
    N, F = features.shape
    T, tile = values.shape[0], values.shape[1]
    tiles = N // tile
    R = lax.axis_size("rows")
    C = lax.axis_size("rep")
    S = R // C
    vmem = pl.BlockSpec(memory_space=pltpu.VMEM)
    anywhere = pl.BlockSpec(memory_space=pltpu.HBM)
    smem = pl.BlockSpec(memory_space=pltpu.SMEM)
    dma = pltpu.SemaphoreType.DMA
    f32, bf16 = jnp.float32, jnp.bfloat16
    sds = jax.ShapeDtypeStruct

    buf, deg_x, deg_o, turned = pl.pallas_call(
        functools.partial(spread_kernel, R, C, S),
        out_shape=(sds((S, N, F), bf16), sds((S, tiles, tile), f32), sds((tiles, tile), f32),
                   sds((T * tile // 2, 2 * tile), f32)),
        in_specs=[anywhere, anywhere, vmem, vmem],
        out_specs=(vmem,) * 4,
        scratch_shapes=[
            pltpu.VMEM((tile, tile, T), bf16), dma((2,)),
            pltpu.VMEM((C, tiles, tile), f32), pltpu.VMEM((tiles, tile), f32),
            dma((S, CHUNKS, 3)), dma((S, CHUNKS)), dma((S, 3)), dma((S,)), dma((C,)), dma((C,))],
        compiler_params=pltpu.CompilerParams(
            collective_id=0, has_side_effects=True, vmem_limit_bytes=32 * 2**20),
    )(features, jnp.transpose(values, (1, 2, 0)), tile_rows[0], tile_count)

    part = pl.pallas_call(
        functools.partial(tile_kernel, C, tiles, tile),
        out_shape=sds((N, F), bf16),
        in_specs=[smem, smem, smem, vmem, vmem, vmem],
        out_specs=vmem,
        scratch_shapes=[pltpu.VMEM(((tiles + 1) * tile, F), f32), pltpu.VMEM((S * N, F), bf16)],
        compiler_params=pltpu.CompilerParams(vmem_limit_bytes=32 * 2**20),
    )(tile_rows[0], tile_cols[0], tile_count, turned, buf, deg_x)

    q = N // C
    share = F // C
    hidden, grad_w, grad_b = pl.pallas_call(
        functools.partial(dense_kernel, R, C),
        out_shape=(sds((C, q, F), bf16), sds((C, share, F), f32), sds((1, F), f32)),
        in_specs=[vmem] * 6,
        out_specs=(vmem,) * 3,
        scratch_shapes=[
            pltpu.VMEM((C, q, F), bf16),
            pltpu.VMEM((C, share + 8, F), f32),
            pltpu.VMEM((C, share + 8, F), f32),
            pltpu.VMEM((R, share + 8, F), f32),
            pltpu.VMEM((share + 8, F), f32),
            dma((C, PARTS)), dma((C, PARTS)), dma((C,)), dma((C,)), dma((C,)), dma((C,)), dma((R,)), dma((R,)),
            dma((C,)), dma((C,))],
        compiler_params=pltpu.CompilerParams(
            collective_id=1, has_side_effects=True, vmem_limit_bytes=32 * 2**20),
    )(part.reshape(C, q, F), features, deg_o, grad_out, weight, bias[None, :])
    return (hidden.reshape(N, F), grad_w.reshape(F, F), grad_b.reshape(F))


def solution(mesh):
    return jax.shard_map(
        local,
        mesh=mesh,
        in_specs=(
            P("rows", None),
            P(),
            P(),
            P("rows", None),
            P("rows", "rep", None, None, None),
            P("rows", "rep", None),
            P("rows", "rep", None),
            P("rows", "rep"),
        ),
        out_specs=(P("rows", None), P(), P()),
        check_vma=False,
    )
```
